32 devices in a mesh: grp: 4 (over x, core), dev: 8 (over z, y).
Axes of the slice: x: 2, y: 2, z: 4, core: 2. Of those that a mesh axis runs over, the one named last changes fastest.
Arguments:
- row_ptr: int32 [4, 33], P('grp'), may hold values from 0 to 1024, as said below
- col_off: int32 [4, 1024], P('grp', 'dev'), may hold values from -24 to 24, as said below
- blocks: bfloat16 [4096, 128, 128], P(('grp', 'dev')), may hold values from -0.09375 to 0.09375
- trial: bfloat16 [16384, 256], P(('grp', 'dev')), may hold values from -6 to 6
Outputs:
- filtered: bfloat16 [24576, 256], P(('grp', 'dev'))
The draws below stay inside these ranges and needn't reach their ends.
Inputs may be any that keep to these rules, and one draw needn't show every extreme that they name: row_ptr[g, 0] = 0 and row_ptr[g, 32] = 1024; every block row holds 24 to 48 nonzero blocks, both reached; in every band the 128 nonzero blocks of some device hold the last blocks of 6 rows. For every device d of a band, the block row that holds nonzero block d * 128 lies between (d - 1) * 4 and (d + 1) * 4. `col_off`: the offsets of one block row are distinct, increasing, and include -24, 0 and 24.
All inputs are finite; a program needn't handle non-finite values.
Results may differ from the reference program's by a relative error of at most 0.0095.
Values may be sent and summed in bfloat16 or wider, within the bound.
A program may use at most 64 MiB of HBM per device.

```python
import jax
import jax.numpy as jnp
import numpy as np
from jax import lax

BLK = 128
M = 256
RB_DEV = 4
AVG = 32
ROW_MIN = 24
ROW_MAX = 48
DEGREE = 2
BAND = 32
HALF = 24
NB = 128
NNZ_DEV = 128
NNZ_BAND = 1024
SPAN = 6
N_GRP = 4
N_DEV = 8


def drawn_rows():
    head_count = 2 * RB_DEV - (SPAN - 1)
    head_sum = 2 * NNZ_DEV - ROW_MIN * (SPAN - 1)
    extra = head_sum - ROW_MIN * head_count
    planted = []
    for position in range(head_count):
        added = min(extra, ROW_MAX - ROW_MIN)
        planted.append(ROW_MIN + added)
        extra = extra - added
    planted = planted + [ROW_MIN] * (SPAN - 1)
    return np.array(planted, dtype=np.int32)


def band_pattern(key):
    devices_band = BAND // RB_DEV
    total_offsets = 2 * HALF + 1
    key_split = jax.random.fold_in(key, 1)
    key_steps = jax.random.fold_in(key, 2)
    key_scores = jax.random.fold_in(key, 3)
    split_at = jax.random.randint(key_split, (), 0, devices_band - 1).astype(jnp.int32)
    row_ids = jnp.arange(BAND, dtype=jnp.int32)
    steps_up = jax.random.randint(key_steps, (BAND,), -4, 5).astype(jnp.int32)
    cut_first = split_at * RB_DEV - 1
    cut_second = (split_at + 2) * RB_DEV - 1
    steps_up = jnp.where((row_ids == cut_first) | (row_ids == cut_second) | (row_ids == BAND - 1), 0, steps_up)
    before = jnp.concatenate([jnp.zeros((1,), jnp.int32), steps_up[:-1]])
    lengths = AVG + steps_up - before
    inside = (row_ids >= split_at * RB_DEV) & (row_ids < (split_at + 2) * RB_DEV)
    planted = jnp.asarray(drawn_rows())
    placed = jnp.take(planted, jnp.clip(row_ids - split_at * RB_DEV, 0, 2 * RB_DEV - 1))
    lengths = jnp.where(inside, placed, lengths).astype(jnp.int32)
    row_ends = jnp.cumsum(lengths).astype(jnp.int32)
    pointer = jnp.concatenate([jnp.zeros((1,), jnp.int32), row_ends])
    offset_ids = jnp.arange(total_offsets, dtype=jnp.int32)
    scores = jax.random.randint(key_scores, (BAND, total_offsets), 0, 1 << 20).astype(jnp.int32) * 256 + offset_ids[None, :]
    forced = (offset_ids == 0) | (offset_ids == HALF) | (offset_ids == 2 * HALF)
    scores = scores + jnp.where(forced, 1 << 29, 0)[None, :]
    ordering = jnp.argsort(-scores, axis=1)
    ranking = jnp.argsort(ordering, axis=1)
    chosen = ranking < lengths[:, None]
    keyed = jnp.where(chosen, offset_ids[None, :], total_offsets + offset_ids[None, :])
    ascending = (jnp.argsort(keyed, axis=1) - HALF).astype(jnp.int32)
    ordinal = jnp.arange(NNZ_BAND, dtype=jnp.int32)
    row_of = jnp.sum((row_ends[None, :] <= ordinal[:, None]).astype(jnp.int32), axis=1)
    place = ordinal - jnp.take(pointer, row_of)
    offsets = jnp.take(ascending.reshape(-1), row_of * total_offsets + place)
    return (pointer.astype(jnp.int32), offsets.astype(jnp.int32))


def pattern(key):

    def one_band(band_id):
        return band_pattern(jax.random.fold_in(key, band_id))
    return jax.vmap(one_band)(jnp.arange(N_GRP, dtype=jnp.int32))


def draw_row_ptr(key, part):
    return pattern(jax.random.fold_in(key, 11))[0]


def draw_col_off(key, part):
    return pattern(jax.random.fold_in(key, 11))[1]


def level_of(stream_key, dims, split, smallest, high):
    def one(axis_at, parts):
        draws = jax.random.uniform(jax.random.fold_in(jax.random.fold_in(stream_key, 6), axis_at), (parts,), jnp.float32, smallest / len(split), high / len(split))
        return jnp.repeat(jnp.exp(draws), dims[axis_at] // parts).reshape((-1,) + (1,) * (len(dims) - axis_at - 1))

    gain = one(*split[0])
    for cut in split[1:]:
        gain = gain * one(*cut)
    return gain


def gaussian(own_key, shape, scale, limit, shards=(), kind=jnp.bfloat16):
    gain = level_of(own_key, shape, shards, -0.22, 0.18) if shards else 1.0
    drawn = jax.random.normal(own_key, shape, jnp.float32) * scale * gain
    return jnp.minimum(jnp.maximum(drawn, -limit), limit).astype(kind)


def setup_inputs(seed: int = 0) -> dict:
    splits = jax.random.split(jax.random.key(seed), 5)
    row_ptr = draw_row_ptr(jax.random.fold_in(splits[4], 71), 0)
    col_off = draw_col_off(jax.random.fold_in(splits[4], 71), 0)
    blocks = gaussian(splits[2], (N_GRP * NNZ_BAND, BLK, BLK), (AVG * BLK) ** -0.5, 0.09375, ((0, 32),))
    trial = gaussian(splits[3], (NB * BLK, M), 1.0, 6.0, ((0, 32),))
    return {"row_ptr": row_ptr, "col_off": col_off, "blocks": blocks, "trial": trial}


filter_center = 0.5
filter_halfwidth = 1.5
piece_rows = 256


def count_ends(row_ends, limits):
    return jnp.sum((row_ends[None, :] <= limits[:, None]).astype(jnp.int32), axis=1)


def band_sums(window, pointer, offsets, matrices):
    row_ends = pointer[1:]
    ordinal = jnp.arange(NNZ_BAND, dtype=jnp.int32)
    row_of = count_ends(row_ends, ordinal)
    wanted = (row_of + offsets + HALF).astype(jnp.int32)
    turns = NNZ_BAND // piece_rows

    def one_turn(running, turn_index):
        offset_rows = (turn_index * piece_rows).astype(jnp.int32)
        columns = lax.dynamic_slice_in_dim(wanted, offset_rows, piece_rows)
        targets = lax.dynamic_slice_in_dim(row_of, offset_rows, piece_rows)
        pieces = lax.dynamic_slice_in_dim(matrices, offset_rows, piece_rows, 0).astype(jnp.float32)
        picked = jnp.take(window, columns, axis=0).astype(jnp.float32)
        products = jnp.einsum("pij,pjm->pim", pieces, picked)
        return running + jax.ops.segment_sum(products, targets, num_segments=BAND), None

    initial = jnp.zeros((BAND, BLK, M), jnp.float32)
    return lax.scan(one_turn, initial, jnp.arange(turns, dtype=jnp.int32))[0]


def reference(row_ptr, col_off, blocks, trial):
    current = trial.reshape(NB, BLK, M)
    matrices = blocks.reshape(N_GRP, NNZ_BAND, BLK, BLK)
    band_ids = jnp.arange(N_GRP, dtype=jnp.int32)

    def product(state):
        def one_band(inputs):
            band_id, pointer, offsets, pieces = inputs
            rows = (band_id * BAND - HALF + jnp.arange(BAND + 2 * HALF, dtype=jnp.int32)) % NB
            window = jnp.take(state, rows.astype(jnp.int32), axis=0)
            return band_sums(window, pointer, offsets, pieces)

        return lax.map(one_band, (band_ids, row_ptr, col_off, matrices)).reshape(NB, BLK, M)

    older = current
    for degree in range(DEGREE):
        row_sums = product(current)
        present = current.astype(jnp.float32)
        if degree == 0:
            updated = (row_sums - filter_center * present) / filter_halfwidth
        else:
            updated = 2.0 * (row_sums - filter_center * present) / filter_halfwidth - older.astype(jnp.float32)
        older = current
        current = lax.optimization_barrier(updated.astype(jnp.bfloat16))

    row_ends = row_ptr[:, 1:]
    marks = jnp.arange(N_DEV + 1, dtype=jnp.int32) * NNZ_DEV
    firsts = jnp.sum((row_ends[:, None, :] <= marks[None, :, None]).astype(jnp.int32), axis=2)
    starting = firsts[:, :-1]
    counted = firsts[:, 1:] - firsts[:, :-1]
    slot_ids = jnp.arange(SPAN, dtype=jnp.int32)
    local_rows = starting[:, :, None] + slot_ids[None, None, :]
    filled = slot_ids[None, None, :] < counted[:, :, None]
    global_rows = band_ids[:, None, None] * BAND + jnp.minimum(local_rows, BAND - 1)
    chosen = jnp.take(current, global_rows.reshape(-1).astype(jnp.int32), axis=0)
    chosen = chosen.reshape(N_GRP, N_DEV, SPAN, BLK, M)
    chosen = jnp.where(filled[:, :, :, None, None], chosen, jnp.zeros((), jnp.bfloat16))
    return chosen.reshape(N_GRP * N_DEV * SPAN * BLK, M)
```

```python
import functools

import jax
import jax.numpy as jnp
from jax import lax
from jax.experimental import pallas as pl
from jax.experimental.pallas import tpu as pltpu
from jax.sharding import PartitionSpec as P

SPAN = 6
CENTER = 0.5
HALFWIDTH = 1.5
FLOOR = 24
DEPTH = 8
VMEM_BYTES = 56 * 1024 * 1024
MESH = pl.DeviceIdType.MESH


def grid_of(n_dev):
    z_count = 1
    while z_count * z_count < n_dev:
        z_count *= 2
    return z_count, n_dev // z_count


def spread(mine, window, rb, n_grp, n_dev, low, high, sems):
    recv_own, recv_side, send_z, send_y, send_side, local_sem = sems
    z_count, y_count = grid_of(n_dev)
    g, d = lax.axis_index("grp"), lax.axis_index("dev")
    z, y = d // y_count, lax.rem(d, y_count)
    after = lax.rem(g + 1, n_grp)
    before = lax.rem(g + n_grp - 1, n_grp)
    sends = []

    def rows(slot, count=rb):
        return window.at[pl.ds(slot * rb, count)]

    def post(cond, src, dst, send_sem, recv_sem, target):
        def make():
            return pltpu.make_async_remote_copy(
                src_ref=src, dst_ref=dst, send_sem=send_sem, recv_sem=recv_sem, device_id=target, device_id_type=MESH
            )

        @pl.when(cond)
        def _():
            make().start()

        sends.append((cond, make))

    def held(s, own):
        return mine if own else rows(n_dev + s)

    def to_sides(cond, s, own):
        src = held(s, own)
        post(cond & (s >= d + n_dev - low), src, rows(s), send_side.at[0, s], recv_side.at[0, s], (after, d))
        post(
            cond & (s <= d + high - 1 - n_dev), src, rows(2 * n_dev + s),
            send_side.at[1, s], recv_side.at[1, s], (before, d),
        )
        post(
            cond & (s == d + high - n_dev), src.at[pl.ds(0, 1)], rows(2 * n_dev + s, 1),
            send_side.at[1, s], recv_side.at[1, s], (before, d),
        )

    def arrived(cond, s):
        @pl.when(cond)
        def _():
            pltpu.make_async_copy(rows(n_dev + s), rows(n_dev + s), recv_own.at[s]).wait()

    def line_step(cond, s, way, own):
        src = held(s, own)
        if way >= 0:
            post(cond & (z < z_count - 1), src, rows(n_dev + s), send_z.at[0, s], recv_own.at[s], (g, d + y_count))
        if way <= 0:
            post(cond & (z > 0), src, rows(n_dev + s), send_z.at[1, s], recv_own.at[s], (g, d - y_count))
        for step in range(1, y_count):
            other = z * y_count + lax.rem(y + step, y_count)
            post(cond, src, rows(n_dev + s), send_y.at[step - 1, s], recv_own.at[s], (g, other))
        to_sides(cond, s, own)

    def around(k):
        if k == 0:
            return [(z >= 0, z, 0)]
        return [(z - k >= 0, z - k, 1), (z + k < z_count, z + k, -1)]

    keep = pltpu.make_async_copy(mine, rows(n_dev + d), local_sem)
    keep.start()

    def across(k):
        for cond, at, _ in around(k):
            at = jnp.clip(at, 0, z_count - 1)
            for step in range(1, y_count):
                s = at * y_count + lax.rem(y + step, y_count)
                arrived(cond, s)
                to_sides(cond, s, False)

    for k in range(z_count):
        for cond, at, way in around(k):
            s = jnp.clip(at, 0, z_count - 1) * y_count + y
            if k > 0:
                arrived(cond, s)
            line_step(cond, s, way, k == 0)
        if k > 0:
            across(k - 1)
    across(z_count - 1)

    for s in range(n_dev):
        @pl.when(s >= d + n_dev - low)
        def _(s=s):
            pltpu.make_async_copy(rows(s), rows(s), recv_side.at[0, s]).wait()

        @pl.when(s <= d + high - 1 - n_dev)
        def _(s=s):
            slot = 2 * n_dev + s
            pltpu.make_async_copy(rows(slot), rows(slot), recv_side.at[1, s]).wait()

        @pl.when(s == d + high - n_dev)
        def _(s=s):
            slot = 2 * n_dev + s
            pltpu.make_async_copy(rows(slot, 1), rows(slot, 1), recv_side.at[1, s]).wait()

    for cond, make in sends:
        @pl.when(cond)
        def _(make=make):
            make().wait_send()
    keep.wait()


def greet(n_grp, n_dev, partials):
    _, y_count = grid_of(n_dev)
    z_count = n_dev // y_count
    g, d = lax.axis_index("grp"), lax.axis_index("dev")
    z, y = d // y_count, lax.rem(d, y_count)
    barrier = pltpu.get_barrier_semaphore()
    expected = jnp.int32(0)
    targets = [
        (z >= 0, (lax.rem(g + 1, n_grp), d)),
        (z >= 0, (lax.rem(g + n_grp - 1, n_grp), d)),
        (z < z_count - 1, (g, d + y_count)),
        (z > 0, (g, d - y_count)),
    ]
    for step in range(1, y_count):
        targets.append((z >= 0, (g, z * y_count + lax.rem(y + step, y_count))))
    if partials:
        for by in (1, 2):
            targets.append((d + by < n_dev, (g, d + by)))
            targets.append((d - by >= 0, (g, d - by)))
    for cond, target in targets:
        @pl.when(cond)
        def _(target=target):
            pl.semaphore_signal(barrier, inc=1, device_id=target, device_id_type=MESH)

        expected = expected + jnp.where(cond, 1, 0)
    pl.semaphore_wait(barrier, expected)


def first_kernel(sizes, trial, window, *sems):
    rb, n_grp, n_dev, low, high = sizes
    greet(n_grp, n_dev, False)
    spread(trial, window, rb, n_grp, n_dev, low, high, sems)


def second_kernel(sizes, left, own, right, trial, window, mine, from_low, from_high, from_far, part_send, part_recv, *sems):
    rb, n_grp, n_dev, low, high = sizes
    greet(n_grp, n_dev, True)
    g, d = lax.axis_index("grp"), lax.axis_index("dev")
    parts = [
        (d < n_dev - 1, d > 0, right.at[pl.ds(0, rb)], from_low, (g, d + 1)),
        (d > 0, d < n_dev - 1, left, from_high, (g, d - 1)),
        (d < n_dev - 2, d > 1, right.at[pl.ds(rb, 1)], from_far, (g, d + 2)),
    ]

    def make(at):
        _, _, src, dst, target = parts[at]
        return pltpu.make_async_remote_copy(
            src_ref=src, dst_ref=dst, send_sem=part_send.at[at], recv_sem=part_recv.at[at],
            device_id=target, device_id_type=MESH,
        )

    for at in range(3):
        @pl.when(parts[at][0])
        def _(at=at):
            make(at).start()
    for at in range(3):
        @pl.when(parts[at][1])
        def _(at=at):
            make(at).wait_recv()
            dst = parts[at][3]
            for row in range(dst.shape[0]):
                own[row] = own[row] + dst[row].astype(jnp.float32)

    for row in range(rb):
        present = trial[row].astype(jnp.float32)
        mine[row] = ((own[row] - CENTER * present) / HALFWIDTH).astype(mine.dtype)
    spread(mine, window, rb, n_grp, n_dev, low, high, sems)
    for at in range(3):
        @pl.when(parts[at][0])
        def _(at=at):
            make(at).wait_send()


def row_sum(starts, ends, columns, blocks, window, at):
    begin, end = starts[at], ends[at]

    def step(i, total):
        lhs, rhs = [], []
        for j in range(DEPTH):
            b = begin + i * DEPTH + j
            valid = b < end
            b = jnp.minimum(b, end - 1)
            block = blocks[b]
            lhs.append(jnp.where(valid, block, jnp.zeros_like(block)))
            rhs.append(window[columns[b]])
        return total + jnp.dot(
            jnp.concatenate(lhs, axis=1), jnp.concatenate(rhs, axis=0), preferred_element_type=jnp.float32
        )

    turns = (end - begin + DEPTH - 1) // DEPTH
    return lax.fori_loop(0, turns, step, jnp.zeros(window.shape[1:], jnp.float32))


def frame_kernel(rb, starts, ends, columns, blocks, window, left, own, right):
    @pl.loop(0, rb)
    def _(row):
        left[row] = row_sum(starts, ends, columns, blocks, window, row).astype(left.dtype)

    @pl.loop(0, rb)
    def _(row):
        own[row] = row_sum(starts, ends, columns, blocks, window, rb + row)

    @pl.loop(0, rb + 1)
    def _(row):
        right[row] = row_sum(starts, ends, columns, blocks, window, 2 * rb + row).astype(right.dtype)


def slots_kernel(starts, ends, columns, places, blocks, window, older, updated, tail):
    tail[0] = row_sum(starts, ends, columns, blocks, window, SPAN).astype(tail.dtype)

    @pl.loop(0, SPAN)
    def _(slot):
        total = row_sum(starts, ends, columns, blocks, window, slot)
        present = window[places[0] + slot].astype(jnp.float32)
        value = 2.0 * (total - CENTER * present) / HALFWIDTH - older[slot].astype(jnp.float32)
        updated[slot] = jnp.where(slot < places[1], value, jnp.zeros_like(value))


def local(n_grp, n_dev, row_ptr, col_off, blocks, trial):
    nnz_here, blk, _ = blocks.shape
    vectors = trial.shape[1]
    pointer = row_ptr[0]
    row_ends = pointer[1:]
    band_rows = row_ends.shape[0]
    rb = band_rows // n_dev
    half = max(FLOOR, band_rows // 2)
    reach = -(-half // rb)
    low, high = 1 + reach, 2 + reach
    z_count, y_count = grid_of(n_dev)
    member = lax.axis_index("dev")
    first_nnz = member * nnz_here

    ordinal = first_nnz + jnp.arange(nnz_here, dtype=jnp.int32)
    row_of = jnp.sum((row_ends[None, :] <= ordinal[:, None]).astype(jnp.int32), axis=1)
    columns = (row_of + col_off[0] + band_rows).astype(jnp.int32)
    first_row = row_of[0]
    finished = jnp.sum(((row_ends > first_nnz) & (row_ends <= first_nnz + nnz_here)).astype(jnp.int32))

    def segments(row_ids):
        inside = (row_ids >= 0) & (row_ids < band_rows)
        safe = jnp.clip(row_ids, 0, band_rows - 1)
        begin = jnp.clip(pointer[safe] - first_nnz, 0, nnz_here)
        end = jnp.clip(row_ends[safe] - first_nnz, 0, nnz_here)
        return jnp.where(inside, begin, 0), jnp.where(inside, end, 0)

    frame_starts, frame_ends = segments((member - 1) * rb + jnp.arange(3 * rb + 1, dtype=jnp.int32))
    slot_ids = jnp.arange(SPAN + 1, dtype=jnp.int32)
    tail_row = first_row + finished
    slot_starts, slot_ends = segments(jnp.where(slot_ids < SPAN, first_row + slot_ids, tail_row))
    slot_ends = jnp.where((slot_ids < finished) | (slot_ids == SPAN), slot_ends, slot_starts)
    places = jnp.stack([first_row + band_rows, finished]).astype(jnp.int32)

    own_rows = trial.reshape(rb, blk, vectors)
    sizes = (rb, n_grp, n_dev, low, high)
    dma = pltpu.SemaphoreType.DMA
    sems = [
        dma((n_dev,)), dma((2, n_dev)), dma((2, n_dev)), dma((max(1, y_count - 1), n_dev)), dma((2, n_dev)), dma,
    ]
    any_spec = pl.BlockSpec(memory_space=pl.ANY)
    vmem = pl.BlockSpec(memory_space=pltpu.VMEM)
    smem = pl.BlockSpec(memory_space=pltpu.SMEM)
    kept = trial.dtype

    def shape(rows, dtype):
        return jax.ShapeDtypeStruct((rows, blk, vectors), dtype)

    def remote(collective_id):
        return pltpu.CompilerParams(
            collective_id=collective_id, has_side_effects=True, vmem_limit_bytes=VMEM_BYTES
        )

    here = pltpu.CompilerParams(vmem_limit_bytes=VMEM_BYTES)
    window = pl.pallas_call(
        functools.partial(first_kernel, sizes),
        out_shape=shape(3 * band_rows, kept),
        in_specs=[any_spec],
        out_specs=any_spec,
        scratch_shapes=sems,
        compiler_params=remote(0),
        name="spread_trial",
    )(own_rows)
    left, own, right = pl.pallas_call(
        functools.partial(frame_kernel, rb),
        out_shape=(shape(rb, kept), shape(rb, jnp.float32), shape(rb + 1, kept)),
        in_specs=[smem] * 3 + [vmem] * 2,
        out_specs=(vmem, vmem, vmem),
        compiler_params=here,
        name="sums_first",
    )(frame_starts, frame_ends, columns, blocks, window)
    older = lax.dynamic_slice_in_dim(window, places[0], SPAN, 0)

    def after_parts(left, own, right, trial, window, total, *rest):
        for row in range(rb):
            total[row] = own[row]
        second_kernel(sizes, left, total, right, trial, window, *rest)

    window = pl.pallas_call(
        after_parts,
        out_shape=shape(3 * band_rows, kept),
        in_specs=[vmem] * 4,
        out_specs=any_spec,
        scratch_shapes=[
            pltpu.VMEM((rb, blk, vectors), jnp.float32),
            pltpu.VMEM((rb, blk, vectors), kept),
            pltpu.VMEM((rb, blk, vectors), kept),
            pltpu.VMEM((rb, blk, vectors), kept),
            pltpu.VMEM((1, blk, vectors), kept),
            dma((3,)),
            dma((3,)),
        ] + sems,
        compiler_params=remote(1),
        name="finish_and_spread",
    )(left, own, right, own_rows)
    updated, tail = pl.pallas_call(
        slots_kernel,
        out_shape=(shape(SPAN, jnp.float32), shape(1, kept)),
        in_specs=[smem] * 4 + [vmem] * 3,
        out_specs=(vmem, vmem),
        compiler_params=here,
        name="sums_second",
    )(slot_starts, slot_ends, columns, places, blocks, window, older)
    carried = lax.ppermute(tail, "dev", [(i, i + 1) for i in range(n_dev - 1)])
    carried = carried.astype(jnp.float32) * (2.0 / HALFWIDTH)
    first_slot = (slot_ids[:SPAN] == 0)[:, None, None]
    result = updated + jnp.where(first_slot, carried, 0.0)
    return result.astype(kept).reshape(SPAN * blk, vectors)


def solution(mesh):
    in_specs = (
        P("grp", None),
        P("grp", "dev"),
        P(("grp", "dev"), None, None),
        P(("grp", "dev"), None),
    )
    step = functools.partial(local, mesh.shape["grp"], mesh.shape["dev"])
    return jax.shard_map(step, mesh=mesh, in_specs=in_specs, out_specs=P(("grp", "dev"), None), check_vma=False)
```

```python
import functools

import jax
import jax.numpy as jnp
from jax import lax
from jax.experimental import pallas as pl
from jax.experimental.pallas import tpu as pltpu
from jax.sharding import PartitionSpec as P

SPAN = 6
CENTER = 0.5
HALFWIDTH = 1.5
FLOOR = 24
DEPTH = 16
CHUNKS = 4
VMEM_BYTES = 56 * 1024 * 1024
MESH = pl.DeviceIdType.MESH


def grid_of(n_dev):
    z_count = 1
    while z_count * z_count < n_dev:
        z_count *= 2
    return z_count, n_dev // z_count


def spread(mine, window, rb, n_grp, n_dev, low, high, sems, prepare=None):
    recv_own, recv_side, send_z, send_y, send_side, local_sem = sems
    z_count, y_count = grid_of(n_dev)
    g, d = lax.axis_index("grp"), lax.axis_index("dev")
    z, y = d // y_count, lax.rem(d, y_count)
    after = lax.rem(g + 1, n_grp)
    before = lax.rem(g + n_grp - 1, n_grp)
    sends = []

    def rows(slot, p=None, count=1):
        return window.at[pl.ds(slot * rb, rb)] if p is None else window.at[pl.ds(slot * rb + p, count)]

    def post(cond, src, dst, send_sem, recv_sem, target):
        @pl.when(cond)
        def _():
            pltpu.make_async_remote_copy(
                src_ref=src, dst_ref=dst, send_sem=send_sem, recv_sem=recv_sem, device_id=target, device_id_type=MESH
            ).start()

    def drain(cond, ref, sem):
        @pl.when(cond)
        def _():
            pltpu.make_async_copy(ref, ref, sem).wait()

    def to_sides(cond, s, p, src):
        post(cond & (s >= d + n_dev - low), src, rows(s, p), send_side.at[0, s], recv_side.at[0, s], (after, d))
        post(
            cond & ((s <= d + high - 1 - n_dev) | ((s == d + high - n_dev) & (p == 0))), src, rows(2 * n_dev + s, p),
            send_side.at[1, s], recv_side.at[1, s], (before, d),
        )

    def line_step(cond, s, p, way, src):
        dst = rows(n_dev + s, p)
        if way >= 0:
            post(cond & (z < z_count - 1), src, dst, send_z.at[0, s], recv_own.at[s, p], (g, d + y_count))
        if way <= 0:
            post(cond & (z > 0), src, dst, send_z.at[1, s], recv_own.at[s, p], (g, d - y_count))
        for step in range(1, y_count):
            other = z * y_count + lax.rem(y + step, y_count)
            post(cond, src, dst, send_y.at[step - 1, s], recv_own.at[s, p], (g, other))
        to_sides(cond, s, p, src)

    def around(k):
        if k == 0:
            return [(z >= 0, z, 0)]
        return [(z - k >= 0, z - k, 1), (z + k < z_count, z + k, -1)]

    def across(k, p):
        for cond, at, _ in around(k):
            at = jnp.clip(at, 0, z_count - 1)
            for step in range(1, y_count):
                s = at * y_count + lax.rem(y + step, y_count)
                drain(cond, rows(n_dev + s, p), recv_own.at[s, p])
                to_sides(cond, s, p, rows(n_dev + s, p))

    @pl.loop(0, rb)
    def _(p):
        if prepare is not None:
            prepare(p)
        line_step(z >= 0, d, p, 0, mine.at[pl.ds(p, 1)])

    keep = pltpu.make_async_copy(mine, rows(n_dev + d), local_sem)
    keep.start()

    for k in range(1, z_count + 1):
        @pl.loop(0, rb)
        def _(p, k=k):
            if k < z_count:
                for cond, at, way in around(k):
                    s = jnp.clip(at, 0, z_count - 1) * y_count + y
                    drain(cond, rows(n_dev + s, p), recv_own.at[s, p])
                    line_step(cond, s, p, way, rows(n_dev + s, p))
            across(k - 1, p)

    @pl.loop(0, n_dev)
    def _(s):
        s_z, s_y = s // y_count, lax.rem(s, y_count)
        low_in, high_in, edge_in = s >= d + n_dev - low, s <= d + high - 1 - n_dev, s == d + high - n_dev
        shard, later = rows(s), rows(2 * n_dev + s)
        one = rows(2 * n_dev + s, 0)
        drain(low_in, shard, recv_side.at[0, s])
        drain(high_in, later, recv_side.at[1, s])
        drain(edge_in, one, recv_side.at[1, s])
        drain(low_in, shard, send_side.at[0, s])
        drain(high_in, later, send_side.at[1, s])
        drain(edge_in, one, send_side.at[1, s])
        mine_line = s_y == y
        drain(mine_line & (s_z <= z) & (z < z_count - 1), shard, send_z.at[0, s])
        drain(mine_line & (s_z >= z) & (z > 0), shard, send_z.at[1, s])
        for step in range(1, y_count):
            drain(mine_line, shard, send_y.at[step - 1, s])

    keep.wait()


def greet(n_grp, n_dev, partials):
    _, y_count = grid_of(n_dev)
    z_count = n_dev // y_count
    g, d = lax.axis_index("grp"), lax.axis_index("dev")
    z, y = d // y_count, lax.rem(d, y_count)
    barrier = pltpu.get_barrier_semaphore()
    expected = jnp.int32(0)
    targets = [
        (z >= 0, (lax.rem(g + 1, n_grp), d)),
        (z >= 0, (lax.rem(g + n_grp - 1, n_grp), d)),
        (z < z_count - 1, (g, d + y_count)),
        (z > 0, (g, d - y_count)),
    ]
    for step in range(1, y_count):
        targets.append((z >= 0, (g, z * y_count + lax.rem(y + step, y_count))))
    if partials:
        for by in (1, 2):
            targets.append((d + by < n_dev, (g, d + by)))
            targets.append((d - by >= 0, (g, d - by)))
    for cond, target in targets:
        @pl.when(cond)
        def _(target=target):
            pl.semaphore_signal(barrier, inc=1, device_id=target, device_id_type=MESH)

        expected = expected + jnp.where(cond, 1, 0)
    pl.semaphore_wait(barrier, expected)


def first_kernel(sizes, trial, window, *sems):
    rb, n_grp, n_dev, low, high = sizes
    greet(n_grp, n_dev, False)
    spread(trial, window, rb, n_grp, n_dev, low, high, sems)


def second_kernel(sizes, left, own, right, trial, window, mine, from_low, from_high, from_far, part_send, part_recv, *sems):
    rb, n_grp, n_dev, low, high = sizes
    greet(n_grp, n_dev, True)
    g, d = lax.axis_index("grp"), lax.axis_index("dev")
    up, down, far = (d < n_dev - 1, d > 0), (d > 0, d < n_dev - 1), (d < n_dev - 2, d > 1)

    def copy(src, dst, at, p, target):
        return pltpu.make_async_remote_copy(
            src_ref=src.at[pl.ds(p if at < 2 else rb, 1)], dst_ref=dst.at[pl.ds(p, 1)],
            send_sem=part_send.at[at, p], recv_sem=part_recv.at[at, p], device_id=target, device_id_type=MESH,
        )

    def to_up(p):
        return copy(right, from_low, 0, p, (g, d + 1))

    def to_down(p):
        return copy(left, from_high, 1, p, (g, d - 1))

    def to_far():
        return copy(right, from_far, 2, 0, (g, d + 2))

    pl.when(far[0])(lambda: to_far().start())

    @pl.loop(0, rb)
    def _(p):
        pl.when(up[0])(lambda: to_up(p).start())
        pl.when(down[0])(lambda: to_down(p).start())

    def prepare(p):
        mine_sum[p] = own[p]

        @pl.when(up[1])
        def _():
            to_up(p).wait_recv()
            mine_sum[p] = mine_sum[p] + from_low[p].astype(jnp.float32)

        @pl.when(down[1])
        def _():
            to_down(p).wait_recv()
            mine_sum[p] = mine_sum[p] + from_high[p].astype(jnp.float32)

        @pl.when(far[1] & (p == 0))
        def _():
            to_far().wait_recv()
            mine_sum[p] = mine_sum[p] + from_far[0].astype(jnp.float32)

        present = trial[p].astype(jnp.float32)
        mine[p] = ((mine_sum[p] - CENTER * present) / HALFWIDTH).astype(mine.dtype)

    mine_sum, sems = sems[0], sems[1:]
    spread(mine, window, rb, n_grp, n_dev, low, high, sems, prepare)

    @pl.loop(0, rb)
    def _(p):
        pl.when(up[0])(lambda: to_up(p).wait_send())
        pl.when(down[0])(lambda: to_down(p).wait_send())

    pl.when(far[0])(lambda: to_far().wait_send())


def fetch(sizes, blocks, window, held, near, sems):
    rb, n_grp, n_dev, low, high = sizes
    d = lax.axis_index("dev")
    base = (n_dev + d - low) * rb
    rows = pltpu.make_async_copy(window.at[pl.ds(base, near.shape[0])], near, sems.at[CHUNKS])
    rows.start()
    size = blocks.shape[0] // CHUNKS

    def part(c):
        here = pl.ds(c * size, size)
        return pltpu.make_async_copy(blocks.at[here], held.at[here], sems.at[c])

    for c in range(CHUNKS):
        part(c).start()
    rows.wait()

    def ready(begin, end):
        for c in range(CHUNKS):
            pl.when((begin <= c * size) & (end > c * size))(lambda: part(c).wait())

    return base, ready


def bounds(pointer, row, first_nnz, nnz_here):
    count = pointer.shape[1] - 1
    at = jnp.clip(row, 0, count - 1)
    begin = jnp.clip(pointer[0, at] - first_nnz, 0, nnz_here)
    end = jnp.clip(pointer[0, at + 1] - first_nnz, 0, nnz_here)
    return begin, jnp.where((row >= 0) & (row < count), end, begin)


def row_sum(begin, end, shift, offsets, held, near):
    def step(i, total):
        lhs, rhs = [], []
        for j in range(DEPTH):
            b = begin + i * DEPTH + j
            valid = b < end
            b = jnp.minimum(b, end - 1)
            block = held[b]
            lhs.append(jnp.where(valid, block, jnp.zeros_like(block)))
            rhs.append(near[offsets[0, b] + shift])
        return total + jnp.dot(
            jnp.concatenate(lhs, axis=1), jnp.concatenate(rhs, axis=0), preferred_element_type=jnp.float32
        )

    turns = (end - begin + DEPTH - 1) // DEPTH
    return lax.fori_loop(0, turns, step, jnp.zeros(near.shape[1:], jnp.float32))


def frame_kernel(sizes, pointer, offsets, blocks, window, left, own, right, held, near, sems):
    rb, n_grp, n_dev, low, high = sizes
    nnz_here = blocks.shape[0]
    d = lax.axis_index("dev")
    base, ready = fetch(sizes, blocks, window, held, near, sems)

    def one(at):
        row = (d - 1) * rb + at
        begin, end = bounds(pointer, row, d * nnz_here, nnz_here)
        ready(begin, end)
        return row_sum(begin, end, row + n_dev * rb - base, offsets, held, near)

    @pl.loop(0, rb)
    def _(at):
        left[at] = one(at).astype(left.dtype)

    @pl.loop(0, rb)
    def _(at):
        own[at] = one(rb + at)

    @pl.loop(0, rb + 1)
    def _(at):
        right[at] = one(2 * rb + at).astype(right.dtype)


def slots_kernel(sizes, pointer, offsets, blocks, window, before, filtered, head, tail, held, near, older, sems):
    rb, n_grp, n_dev, low, high = sizes
    nnz_here = blocks.shape[0]
    d = lax.axis_index("dev")
    first_nnz = d * nnz_here
    band_rows = pointer.shape[1] - 1

    def count(limit):
        def add(r, total):
            return total + jnp.where(pointer[0, r + 1] <= limit, 1, 0)

        return lax.fori_loop(0, band_rows, add, jnp.int32(0))

    first = count(first_nnz)
    finished = count(first_nnz + nnz_here) - first
    past = pltpu.make_async_copy(before.at[pl.ds(band_rows + first, SPAN)], older, sems.at[CHUNKS + 1])
    past.start()
    base, ready = fetch(sizes, blocks, window, held, near, sems)
    past.wait()

    def one(row):
        begin, end = bounds(pointer, row, first_nnz, nnz_here)
        ready(begin, end)
        return row_sum(begin, end, row + band_rows - base, offsets, held, near)

    @pl.loop(0, SPAN)
    def _(slot):
        filled = slot < finished
        row = first + slot

        @pl.when(filled)
        def _():
            present = near[row + band_rows - base].astype(jnp.float32)
            value = 2.0 * (one(row) - CENTER * present) / HALFWIDTH - older[slot].astype(jnp.float32)
            filtered[slot] = value.astype(filtered.dtype)

            @pl.when(slot == 0)
            def _():
                head[0] = value

        @pl.when(jnp.logical_not(filled))
        def _():
            filtered[slot] = jnp.zeros(filtered.shape[1:], filtered.dtype)

    tail[0] = one(first + finished).astype(tail.dtype)


def local(n_grp, n_dev, row_ptr, col_off, blocks, trial):
    nnz_here, blk, _ = blocks.shape
    vectors = trial.shape[1]
    band_rows = row_ptr.shape[1] - 1
    rb = band_rows // n_dev
    half = max(FLOOR, band_rows // 2)
    reach = -(-half // rb)
    low, high = 1 + reach, 2 + reach
    _, y_count = grid_of(n_dev)
    own_rows = trial.reshape(rb, blk, vectors)
    sizes = (rb, n_grp, n_dev, low, high)
    near_rows = (low + high) * rb + 1
    dma = pltpu.SemaphoreType.DMA
    sems = [
        dma((n_dev, rb)), dma((2, n_dev)), dma((2, n_dev)), dma((max(1, y_count - 1), n_dev)), dma((2, n_dev)), dma,
    ]
    any_spec = pl.BlockSpec(memory_space=pl.ANY)
    vmem = pl.BlockSpec(memory_space=pltpu.VMEM)
    smem = pl.BlockSpec(memory_space=pltpu.SMEM)
    kept = trial.dtype

    def shape(rows, dtype):
        return jax.ShapeDtypeStruct((rows, blk, vectors), dtype)

    def buffer(rows, dtype):
        return pltpu.VMEM((rows, blk, vectors), dtype)

    def remote(collective_id):
        return pltpu.CompilerParams(
            collective_id=collective_id, has_side_effects=True, vmem_limit_bytes=VMEM_BYTES
        )

    here = pltpu.CompilerParams(vmem_limit_bytes=VMEM_BYTES)
    first = pl.pallas_call(
        functools.partial(first_kernel, sizes),
        out_shape=shape(3 * band_rows, kept),
        in_specs=[any_spec],
        out_specs=any_spec,
        scratch_shapes=sems,
        compiler_params=remote(0),
        name="spread_trial",
    )(own_rows)
    left, own, right = pl.pallas_call(
        functools.partial(frame_kernel, sizes),
        out_shape=(shape(rb, kept), shape(rb, jnp.float32), shape(rb + 1, kept)),
        in_specs=[smem] * 2 + [any_spec] * 2,
        out_specs=(vmem, vmem, vmem),
        scratch_shapes=[pltpu.VMEM(blocks.shape, blocks.dtype), buffer(near_rows, kept), dma((CHUNKS + 1,))],
        compiler_params=here,
        name="sums_first",
    )(row_ptr, col_off, blocks, first)
    second = pl.pallas_call(
        functools.partial(second_kernel, sizes),
        out_shape=shape(3 * band_rows, kept),
        in_specs=[vmem] * 4,
        out_specs=any_spec,
        scratch_shapes=[buffer(rb, kept)] * 3 + [buffer(1, kept), dma((3, rb)), dma((3, rb)), buffer(rb, jnp.float32)] + sems,
        compiler_params=remote(1),
        name="finish_and_spread",
    )(left, own, right, own_rows)
    filtered, head, tail = pl.pallas_call(
        functools.partial(slots_kernel, sizes),
        out_shape=(shape(SPAN, kept), shape(1, jnp.float32), shape(1, kept)),
        in_specs=[smem] * 2 + [any_spec] * 3,
        out_specs=(vmem, vmem, vmem),
        scratch_shapes=[
            pltpu.VMEM(blocks.shape, blocks.dtype), buffer(near_rows, kept), buffer(SPAN, kept), dma((CHUNKS + 2,)),
        ],
        compiler_params=here,
        name="sums_second",
    )(row_ptr, col_off, blocks, second, first)
    carried = lax.ppermute(tail, "dev", [(i, i + 1) for i in range(n_dev - 1)])
    start = (head + carried.astype(jnp.float32) * (2.0 / HALFWIDTH)).astype(kept)
    filtered = lax.dynamic_update_slice_in_dim(filtered, start, 0, 0)
    return filtered.reshape(SPAN * blk, vectors)


def solution(mesh):
    in_specs = (
        P("grp", None),
        P("grp", "dev"),
        P(("grp", "dev"), None, None),
        P(("grp", "dev"), None),
    )
    step = functools.partial(local, mesh.shape["grp"], mesh.shape["dev"])
    return jax.shard_map(step, mesh=mesh, in_specs=in_specs, out_specs=P(("grp", "dev"), None), check_vma=False)
```

```python
import functools

import jax
import jax.numpy as jnp
from jax import lax
from jax.experimental import pallas as pl
from jax.experimental.pallas import tpu as pltpu
from jax.sharding import PartitionSpec as P

SPAN = 6
CENTER = 0.5
HALFWIDTH = 1.5
FLOOR = 24
ROW_MAX = 48
DEPTH = 16
CHUNKS = 4
VMEM_BYTES = 56 * 1024 * 1024
MESH = pl.DeviceIdType.MESH


def grid_of(n_dev):
    z_count = 1
    while z_count * z_count < n_dev:
        z_count *= 2
    return z_count, n_dev // z_count


def spread(mine, window, rb, n_grp, n_dev, low, high, sems, prepare=None):
    recv_own, recv_side, send_z, send_y, send_side, local_sem = sems
    z_count, y_count = grid_of(n_dev)
    g, d = lax.axis_index("grp"), lax.axis_index("dev")
    z, y = d // y_count, lax.rem(d, y_count)
    after = lax.rem(g + 1, n_grp)
    before = lax.rem(g + n_grp - 1, n_grp)
    early = max(1, rb // 4) if y_count > 1 else 0

    def rows(slot, p=None, count=1):
        return window.at[pl.ds(slot * rb, rb)] if p is None else window.at[pl.ds(slot * rb + p, count)]

    def post(cond, src, dst, send_sem, recv_sem, target):
        @pl.when(cond)
        def _():
            pltpu.make_async_remote_copy(
                src_ref=src, dst_ref=dst, send_sem=send_sem, recv_sem=recv_sem, device_id=target, device_id_type=MESH
            ).start()

    def drain(cond, ref, sem):
        @pl.when(cond)
        def _():
            pltpu.make_async_copy(ref, ref, sem).wait()

    def to_sides(cond, s, p, src):
        post(cond & (s >= d + n_dev - low), src, rows(s, p), send_side.at[0, s], recv_side.at[0, s], (after, d))
        post(
            cond & ((s <= d + high - 1 - n_dev) | ((s == d + high - n_dev) & (p == 0))), src, rows(2 * n_dev + s, p),
            send_side.at[1, s], recv_side.at[1, s], (before, d),
        )

    def along(cond, s, p, way, src):
        dst = rows(n_dev + s, p)
        if way >= 0:
            post(cond & (z < z_count - 1), src, dst, send_z.at[0, s], recv_own.at[s, p], (g, d + y_count))
        if way <= 0:
            post(cond & (z > 0), src, dst, send_z.at[1, s], recv_own.at[s, p], (g, d - y_count))

    def line_step(cond, s, p, way, src):
        along(cond, s, p, way, src)
        for step in range(1, y_count):
            other = z * y_count + lax.rem(y + step, y_count)
            post(
                cond if way == 0 else cond & (p >= early), src, rows(n_dev + s, p),
                send_y.at[step - 1, s], recv_own.at[s, p], (g, other),
            )
        to_sides(cond, s, p, src)

    def around(k):
        if k == 0:
            return [(z >= 0, z, 0)]
        return [(z - k >= 0, z - k, 1), (z + k < z_count, z + k, -1)]

    def across(k, p):
        for cond, at, way in around(k):
            at = jnp.clip(at, 0, z_count - 1)
            for step in range(1, y_count):
                s = at * y_count + lax.rem(y + step, y_count)
                drain(cond, rows(n_dev + s, p), recv_own.at[s, p])
                along(cond & (p < early), s, p, way, rows(n_dev + s, p))
                to_sides(cond, s, p, rows(n_dev + s, p))

    @pl.loop(0, rb)
    def _(p):
        if prepare is not None:
            prepare(p)
        line_step(z >= 0, d, p, 0, mine.at[pl.ds(p, 1)])

    keep = pltpu.make_async_copy(mine, rows(n_dev + d), local_sem)
    keep.start()

    for k in range(1, z_count + 1):
        @pl.loop(0, rb)
        def _(p, k=k):
            if k < z_count:
                for cond, at, way in around(k):
                    s = jnp.clip(at, 0, z_count - 1) * y_count + y
                    drain(cond, rows(n_dev + s, p), recv_own.at[s, p])
                    line_step(cond, s, p, way, rows(n_dev + s, p))
            across(k - 1, p)

    @pl.loop(0, n_dev)
    def _(s):
        s_z, s_y = s // y_count, lax.rem(s, y_count)
        low_in, high_in, edge_in = s >= d + n_dev - low, s <= d + high - 1 - n_dev, s == d + high - n_dev
        shard, later = rows(s), rows(2 * n_dev + s)
        one = rows(2 * n_dev + s, 0)
        drain(low_in, shard, recv_side.at[0, s])
        drain(high_in, later, recv_side.at[1, s])
        drain(edge_in, one, recv_side.at[1, s])
        drain(low_in, shard, send_side.at[0, s])
        drain(high_in, later, send_side.at[1, s])
        drain(edge_in, one, send_side.at[1, s])
        first, rest = window.at[pl.ds(s * rb, max(1, early))], window.at[pl.ds(s * rb, rb - early)]
        line = s_y == y
        for way, cond in ((0, (s_z <= z) & (z < z_count - 1)), (1, (s_z >= z) & (z > 0))):
            drain(cond & line, shard, send_z.at[way, s])
            if early:
                drain(cond & jnp.logical_not(line), first, send_z.at[way, s])
        for step in range(1, y_count):
            drain(s == d, shard, send_y.at[step - 1, s])
            drain(line & (s != d), rest, send_y.at[step - 1, s])

    keep.wait()


def greet(n_grp, n_dev, partials):
    _, y_count = grid_of(n_dev)
    z_count = n_dev // y_count
    g, d = lax.axis_index("grp"), lax.axis_index("dev")
    z, y = d // y_count, lax.rem(d, y_count)
    barrier = pltpu.get_barrier_semaphore()
    expected = jnp.int32(0)
    targets = [
        (z >= 0, (lax.rem(g + 1, n_grp), d)),
        (z >= 0, (lax.rem(g + n_grp - 1, n_grp), d)),
        (z < z_count - 1, (g, d + y_count)),
        (z > 0, (g, d - y_count)),
    ]
    for step in range(1, y_count):
        targets.append((z >= 0, (g, z * y_count + lax.rem(y + step, y_count))))
    if partials:
        for by in (1, 2):
            targets.append((d + by < n_dev, (g, d + by)))
            targets.append((d - by >= 0, (g, d - by)))
    for cond, target in targets:
        @pl.when(cond)
        def _(target=target):
            pl.semaphore_signal(barrier, inc=1, device_id=target, device_id_type=MESH)

        expected = expected + jnp.where(cond, 1, 0)
    pl.semaphore_wait(barrier, expected)


def first_kernel(sizes, trial, window, *sems):
    rb, n_grp, n_dev, low, high = sizes
    greet(n_grp, n_dev, False)
    spread(trial, window, rb, n_grp, n_dev, low, high, sems)


def second_kernel(sizes, left, own, right, trial, window, mine, from_low, from_high, from_far, part_send, part_recv, *sems):
    rb, n_grp, n_dev, low, high = sizes
    greet(n_grp, n_dev, True)
    g, d = lax.axis_index("grp"), lax.axis_index("dev")
    up, down, far = (d < n_dev - 1, d > 0), (d > 0, d < n_dev - 1), (d < n_dev - 2, d > 1)

    def copy(src, dst, at, p, target):
        return pltpu.make_async_remote_copy(
            src_ref=src.at[pl.ds(p if at < 2 else rb, 1)], dst_ref=dst.at[pl.ds(p, 1)],
            send_sem=part_send.at[at, p], recv_sem=part_recv.at[at, p], device_id=target, device_id_type=MESH,
        )

    def to_up(p):
        return copy(right, from_low, 0, p, (g, d + 1))

    def to_down(p):
        return copy(left, from_high, 1, p, (g, d - 1))

    def to_far():
        return copy(right, from_far, 2, 0, (g, d + 2))

    pl.when(far[0])(lambda: to_far().start())

    @pl.loop(0, rb)
    def _(p):
        pl.when(up[0])(lambda: to_up(p).start())
        pl.when(down[0])(lambda: to_down(p).start())

    def prepare(p):
        mine_sum[p] = own[p]

        @pl.when(up[1])
        def _():
            to_up(p).wait_recv()
            mine_sum[p] = mine_sum[p] + from_low[p].astype(jnp.float32)

        @pl.when(down[1])
        def _():
            to_down(p).wait_recv()
            mine_sum[p] = mine_sum[p] + from_high[p].astype(jnp.float32)

        @pl.when(far[1] & (p == 0))
        def _():
            to_far().wait_recv()
            mine_sum[p] = mine_sum[p] + from_far[0].astype(jnp.float32)

        present = trial[p].astype(jnp.float32)
        mine[p] = ((mine_sum[p] - CENTER * present) / HALFWIDTH).astype(mine.dtype)

    mine_sum, sems = sems[0], sems[1:]
    spread(mine, window, rb, n_grp, n_dev, low, high, sems, prepare)

    @pl.loop(0, rb)
    def _(p):
        pl.when(up[0])(lambda: to_up(p).wait_send())
        pl.when(down[0])(lambda: to_down(p).wait_send())

    pl.when(far[0])(lambda: to_far().wait_send())


def fetch(sizes, blocks, window, held, near, sems):
    rb, n_grp, n_dev, low, high = sizes
    d = lax.axis_index("dev")
    base = (n_dev + d - low) * rb
    rows = pltpu.make_async_copy(window.at[pl.ds(base, near.shape[0])], near, sems.at[CHUNKS])
    rows.start()
    size = blocks.shape[0] // CHUNKS

    def part(c):
        here = pl.ds(c * size, size)
        return pltpu.make_async_copy(blocks.at[here], held.at[here], sems.at[c])

    for c in range(CHUNKS):
        part(c).start()
    rows.wait()

    def ready(begin, end):
        for c in range(CHUNKS):
            pl.when((begin <= c * size) & (end > c * size))(lambda: part(c).wait())

    return base, ready


def bounds(pointer, row, first_nnz, nnz_here):
    count = pointer.shape[1] - 1
    at = jnp.clip(row, 0, count - 1)
    begin = jnp.clip(pointer[0, at] - first_nnz, 0, nnz_here)
    end = jnp.clip(pointer[0, at + 1] - first_nnz, 0, nnz_here)
    return begin, jnp.where((row >= 0) & (row < count), end, begin)


def row_sum(begin, end, shift, offsets, held, near, skipped=0):
    def step(i, total):
        lhs, rhs = [], []
        for j in range(DEPTH):
            b = begin + i * DEPTH + j
            valid = b < end
            b = jnp.minimum(b, end - 1)
            block = held[b - skipped]
            lhs.append(jnp.where(valid, block, jnp.zeros_like(block)))
            rhs.append(near[offsets[0, b] + shift])
        return total + jnp.dot(
            jnp.concatenate(lhs, axis=1), jnp.concatenate(rhs, axis=0), preferred_element_type=jnp.float32
        )

    turns = (end - begin + DEPTH - 1) // DEPTH
    return lax.fori_loop(0, turns, step, jnp.zeros(near.shape[1:], jnp.float32))


def frame_kernel(sizes, pointer, offsets, blocks, window, left, own, right, held, near, sems):
    rb, n_grp, n_dev, low, high = sizes
    nnz_here = blocks.shape[0]
    d = lax.axis_index("dev")
    base, ready = fetch(sizes, blocks, window, held, near, sems)

    def one(at):
        row = (d - 1) * rb + at
        begin, end = bounds(pointer, row, d * nnz_here, nnz_here)
        ready(begin, end)
        return row_sum(begin, end, row + n_dev * rb - base, offsets, held, near)

    @pl.loop(0, rb)
    def _(at):
        left[at] = one(at).astype(left.dtype)

    @pl.loop(0, rb)
    def _(at):
        own[at] = one(rb + at)

    @pl.loop(0, rb + 1)
    def _(at):
        right[at] = one(2 * rb + at).astype(right.dtype)


def rows_ended(pointer, limit):
    def add(r, total):
        return total + jnp.where(pointer[0, r + 1] <= limit, 1, 0)

    return lax.fori_loop(0, pointer.shape[1] - 1, add, jnp.int32(0))


def tail_kernel(sizes, pointer, offsets, blocks, window, tail, held, near, sems):
    rb, n_grp, n_dev, low, high = sizes
    nnz_here = blocks.shape[0]
    skipped = nnz_here - held.shape[0]
    d = lax.axis_index("dev")
    row = rows_ended(pointer, (d + 1) * nnz_here)
    reach = high - 2
    base = (n_dev - reach) * rb + row
    base = jnp.minimum(base, (n_dev + d + high) * rb + 1 - near.shape[0])
    some = pltpu.make_async_copy(blocks.at[pl.ds(skipped, held.shape[0])], held, sems.at[0])
    some.start()
    rows = pltpu.make_async_copy(window.at[pl.ds(base, near.shape[0])], near, sems.at[1])
    rows.start()
    begin, end = bounds(pointer, row, d * nnz_here, nnz_here)
    some.wait()
    rows.wait()
    tail[0] = row_sum(begin, end, row + n_dev * rb - base, offsets, held, near, skipped).astype(tail.dtype)


def slots_kernel(sizes, pointer, offsets, blocks, window, before, filtered, head, held, near, older, sems):
    rb, n_grp, n_dev, low, high = sizes
    nnz_here = blocks.shape[0]
    d = lax.axis_index("dev")
    first_nnz = d * nnz_here
    band_rows = pointer.shape[1] - 1

    first = rows_ended(pointer, first_nnz)
    finished = rows_ended(pointer, first_nnz + nnz_here) - first
    past = pltpu.make_async_copy(before.at[pl.ds(band_rows + first, SPAN)], older, sems.at[CHUNKS + 1])
    past.start()
    base, ready = fetch(sizes, blocks, window, held, near, sems)
    past.wait()

    def one(row):
        begin, end = bounds(pointer, row, first_nnz, nnz_here)
        ready(begin, end)
        return row_sum(begin, end, row + band_rows - base, offsets, held, near)

    @pl.loop(0, SPAN)
    def _(slot):
        filled = slot < finished
        row = first + slot

        @pl.when(filled)
        def _():
            present = near[row + band_rows - base].astype(jnp.float32)
            value = 2.0 * (one(row) - CENTER * present) / HALFWIDTH - older[slot].astype(jnp.float32)
            filtered[slot] = value.astype(filtered.dtype)

            @pl.when(slot == 0)
            def _():
                head[0] = value

        @pl.when(jnp.logical_not(filled))
        def _():
            filtered[slot] = jnp.zeros(filtered.shape[1:], filtered.dtype)

    ready(*bounds(pointer, first + finished, first_nnz, nnz_here))


def local(n_grp, n_dev, row_ptr, col_off, blocks, trial):
    nnz_here, blk, _ = blocks.shape
    vectors = trial.shape[1]
    band_rows = row_ptr.shape[1] - 1
    rb = band_rows // n_dev
    half = max(FLOOR, band_rows // 2)
    reach = -(-half // rb)
    low, high = 1 + reach, 2 + reach
    _, y_count = grid_of(n_dev)
    own_rows = trial.reshape(rb, blk, vectors)
    sizes = (rb, n_grp, n_dev, low, high)
    near_rows = (low + high) * rb + 1
    dma = pltpu.SemaphoreType.DMA
    sems = [
        dma((n_dev, rb)), dma((2, n_dev)), dma((2, n_dev)), dma((max(1, y_count - 1), n_dev)), dma((2, n_dev)), dma,
    ]
    any_spec = pl.BlockSpec(memory_space=pl.ANY)
    vmem = pl.BlockSpec(memory_space=pltpu.VMEM)
    smem = pl.BlockSpec(memory_space=pltpu.SMEM)
    kept = trial.dtype

    def shape(rows, dtype):
        return jax.ShapeDtypeStruct((rows, blk, vectors), dtype)

    def buffer(rows, dtype):
        return pltpu.VMEM((rows, blk, vectors), dtype)

    def remote(collective_id):
        return pltpu.CompilerParams(
            collective_id=collective_id, has_side_effects=True, vmem_limit_bytes=VMEM_BYTES
        )

    here = pltpu.CompilerParams(vmem_limit_bytes=VMEM_BYTES)
    first = pl.pallas_call(
        functools.partial(first_kernel, sizes),
        out_shape=shape(3 * band_rows, kept),
        in_specs=[any_spec],
        out_specs=any_spec,
        scratch_shapes=sems,
        compiler_params=remote(0),
        name="spread_trial",
    )(own_rows)
    left, own, right = pl.pallas_call(
        functools.partial(frame_kernel, sizes),
        out_shape=(shape(rb, kept), shape(rb, jnp.float32), shape(rb + 1, kept)),
        in_specs=[smem] * 2 + [any_spec] * 2,
        out_specs=(vmem, vmem, vmem),
        scratch_shapes=[pltpu.VMEM(blocks.shape, blocks.dtype), buffer(near_rows, kept), dma((CHUNKS + 1,))],
        compiler_params=here,
        name="sums_first",
    )(row_ptr, col_off, blocks, first)
    second = pl.pallas_call(
        functools.partial(second_kernel, sizes),
        out_shape=shape(3 * band_rows, kept),
        in_specs=[vmem] * 4,
        out_specs=any_spec,
        scratch_shapes=[buffer(rb, kept)] * 3 + [buffer(1, kept), dma((3, rb)), dma((3, rb)), buffer(rb, jnp.float32)] + sems,
        compiler_params=remote(1),
        name="finish_and_spread",
    )(left, own, right, own_rows)
    tail_blocks = min(ROW_MAX, nnz_here)
    tail = pl.pallas_call(
        functools.partial(tail_kernel, sizes),
        out_shape=shape(1, kept),
        in_specs=[smem] * 2 + [any_spec] * 2,
        out_specs=vmem,
        scratch_shapes=[pltpu.VMEM((tail_blocks,) + blocks.shape[1:], blocks.dtype), buffer(2 * reach * rb + 1, kept), dma((2,))],
        compiler_params=here,
        cost_estimate=pl.CostEstimate(
            flops=2 * tail_blocks * blk * blk * vectors, bytes_accessed=2 * blk * (tail_blocks * blk + (2 * reach * rb + 1) * vectors),
            transcendentals=0,
        ),
        name="tail_sum",
    )(row_ptr, col_off, blocks, second)
    carried = lax.ppermute(tail, "dev", [(i, i + 1) for i in range(n_dev - 1)])
    filtered, head = pl.pallas_call(
        functools.partial(slots_kernel, sizes),
        out_shape=(shape(SPAN, kept), shape(1, jnp.float32)),
        in_specs=[smem] * 2 + [any_spec] * 3,
        out_specs=(vmem, vmem),
        scratch_shapes=[
            pltpu.VMEM(blocks.shape, blocks.dtype), buffer(near_rows, kept), buffer(SPAN, kept), dma((CHUNKS + 2,)),
        ],
        compiler_params=here,
        cost_estimate=pl.CostEstimate(
            flops=8 * nnz_here * blk * blk * vectors, bytes_accessed=2 * blk * (nnz_here * blk + near_rows * vectors),
            transcendentals=0,
        ),
        name="sums_second",
    )(row_ptr, col_off, blocks, second, first)
    start = (head + carried.astype(jnp.float32) * (2.0 / HALFWIDTH)).astype(kept)
    filtered = lax.dynamic_update_slice_in_dim(filtered, start, 0, 0)
    return filtered.reshape(SPAN * blk, vectors)


def solution(mesh):
    in_specs = (
        P("grp", None),
        P("grp", "dev"),
        P(("grp", "dev"), None, None),
        P(("grp", "dev"), None),
    )
    step = functools.partial(local, mesh.shape["grp"], mesh.shape["dev"])
    return jax.shard_map(step, mesh=mesh, in_specs=in_specs, out_specs=P(("grp", "dev"), None), check_vma=False)
```

```python
import functools

import jax
import jax.numpy as jnp
from jax import lax
from jax.experimental import pallas as pl
from jax.experimental.pallas import tpu as pltpu
from jax.sharding import PartitionSpec as P

SPAN = 6
CENTER = 0.5
HALFWIDTH = 1.5
FLOOR = 24
DEPTH = 16
CHUNKS = 4
VMEM_BYTES = 56 * 1024 * 1024
MESH = pl.DeviceIdType.MESH


def grid_of(n_dev):
    z_count = 1
    while z_count * z_count < n_dev:
        z_count *= 2
    return z_count, n_dev // z_count


def spread(mine, window, rb, n_grp, n_dev, low, high, sems, prepare=None):
    recv_own, recv_side, send_z, send_y, send_side, local_sem = sems
    z_count, y_count = grid_of(n_dev)
    g, d = lax.axis_index("grp"), lax.axis_index("dev")
    z, y = d // y_count, lax.rem(d, y_count)
    after = lax.rem(g + 1, n_grp)
    before = lax.rem(g + n_grp - 1, n_grp)
    early = rb // 4 if y_count > 1 and prepare is not None else 0

    def rows(slot, p=None, count=1):
        return window.at[pl.ds(slot * rb, rb)] if p is None else window.at[pl.ds(slot * rb + p, count)]

    def post(cond, src, dst, send_sem, recv_sem, target):
        @pl.when(cond)
        def _():
            pltpu.make_async_remote_copy(
                src_ref=src, dst_ref=dst, send_sem=send_sem, recv_sem=recv_sem, device_id=target, device_id_type=MESH
            ).start()

    def drain(cond, ref, sem):
        @pl.when(cond)
        def _():
            pltpu.make_async_copy(ref, ref, sem).wait()

    def to_sides(cond, s, p, src):
        post(cond & (s >= d + n_dev - low), src, rows(s, p), send_side.at[0, s], recv_side.at[0, s], (after, d))
        post(
            cond & ((s <= d + high - 1 - n_dev) | ((s == d + high - n_dev) & (p == 0))), src, rows(2 * n_dev + s, p),
            send_side.at[1, s], recv_side.at[1, s], (before, d),
        )

    def along(cond, s, p, way, src):
        dst = rows(n_dev + s, p)
        if way >= 0:
            post(cond & (z < z_count - 1), src, dst, send_z.at[0, s], recv_own.at[s, p], (g, d + y_count))
        if way <= 0:
            post(cond & (z > 0), src, dst, send_z.at[1, s], recv_own.at[s, p], (g, d - y_count))

    def line_step(cond, s, p, way, src):
        along(cond, s, p, way, src)
        for step in range(1, y_count):
            other = z * y_count + lax.rem(y + step, y_count)
            post(
                cond if way == 0 else cond & (p >= early), src, rows(n_dev + s, p),
                send_y.at[step - 1, s], recv_own.at[s, p], (g, other),
            )
        to_sides(cond, s, p, src)

    def around(k):
        if k == 0:
            return [(z >= 0, z, 0)]
        return [(z - k >= 0, z - k, 1), (z + k < z_count, z + k, -1)]

    def across(k, p):
        for cond, at, way in around(k):
            at = jnp.clip(at, 0, z_count - 1)
            for step in range(1, y_count):
                s = at * y_count + lax.rem(y + step, y_count)
                drain(cond, rows(n_dev + s, p), recv_own.at[s, p])
                along(cond & (p < early), s, p, way, rows(n_dev + s, p))
                to_sides(cond, s, p, rows(n_dev + s, p))

    @pl.loop(0, rb)
    def _(p):
        if prepare is not None:
            prepare(p)
        line_step(z >= 0, d, p, 0, mine.at[pl.ds(p, 1)])

    keep = pltpu.make_async_copy(mine, rows(n_dev + d), local_sem)
    keep.start()

    for k in range(1, z_count + 1):
        @pl.loop(0, rb)
        def _(p, k=k):
            if k < z_count:
                for cond, at, way in around(k):
                    s = jnp.clip(at, 0, z_count - 1) * y_count + y
                    drain(cond, rows(n_dev + s, p), recv_own.at[s, p])
                    line_step(cond, s, p, way, rows(n_dev + s, p))
            across(k - 1, p)

    @pl.loop(0, n_dev)
    def _(s):
        s_z, s_y = s // y_count, lax.rem(s, y_count)
        low_in, high_in, edge_in = s >= d + n_dev - low, s <= d + high - 1 - n_dev, s == d + high - n_dev
        shard, later = rows(s), rows(2 * n_dev + s)
        one = rows(2 * n_dev + s, 0)
        drain(low_in, shard, recv_side.at[0, s])
        drain(high_in, later, recv_side.at[1, s])
        drain(edge_in, one, recv_side.at[1, s])
        drain(low_in, shard, send_side.at[0, s])
        drain(high_in, later, send_side.at[1, s])
        drain(edge_in, one, send_side.at[1, s])
        first, rest = window.at[pl.ds(s * rb, max(1, early))], window.at[pl.ds(s * rb, rb - early)]
        line = s_y == y
        for way, cond in ((0, (s_z <= z) & (z < z_count - 1)), (1, (s_z >= z) & (z > 0))):
            drain(cond & line, shard, send_z.at[way, s])
            if early:
                drain(cond & jnp.logical_not(line), first, send_z.at[way, s])
        for step in range(1, y_count):
            drain(s == d, shard, send_y.at[step - 1, s])
            drain(line & (s != d), rest, send_y.at[step - 1, s])

    keep.wait()


def greet(n_grp, n_dev, partials):
    _, y_count = grid_of(n_dev)
    z_count = n_dev // y_count
    g, d = lax.axis_index("grp"), lax.axis_index("dev")
    z, y = d // y_count, lax.rem(d, y_count)
    barrier = pltpu.get_barrier_semaphore()
    expected = jnp.int32(0)
    targets = [
        (z >= 0, (lax.rem(g + 1, n_grp), d)),
        (z >= 0, (lax.rem(g + n_grp - 1, n_grp), d)),
        (z < z_count - 1, (g, d + y_count)),
        (z > 0, (g, d - y_count)),
    ]
    for step in range(1, y_count):
        targets.append((z >= 0, (g, z * y_count + lax.rem(y + step, y_count))))
    if partials:
        for by in (1, 2):
            targets.append((d + by < n_dev, (g, d + by)))
            targets.append((d - by >= 0, (g, d - by)))
    for cond, target in targets:
        @pl.when(cond)
        def _(target=target):
            pl.semaphore_signal(barrier, inc=1, device_id=target, device_id_type=MESH)

        expected = expected + jnp.where(cond, 1, 0)
    pl.semaphore_wait(barrier, expected)


def first_kernel(sizes, trial, window, *sems):
    rb, n_grp, n_dev, low, high = sizes
    greet(n_grp, n_dev, False)
    spread(trial, window, rb, n_grp, n_dev, low, high, sems)


def second_kernel(sizes, left, own, right, trial, window, mine, from_low, from_high, from_far, part_send, part_recv, *sems):
    rb, n_grp, n_dev, low, high = sizes
    greet(n_grp, n_dev, True)
    g, d = lax.axis_index("grp"), lax.axis_index("dev")
    up, down, far = (d < n_dev - 1, d > 0), (d > 0, d < n_dev - 1), (d < n_dev - 2, d > 1)

    def copy(src, dst, at, p, target):
        return pltpu.make_async_remote_copy(
            src_ref=src.at[pl.ds(p if at < 2 else rb, 1)], dst_ref=dst.at[pl.ds(p, 1)],
            send_sem=part_send.at[at, p], recv_sem=part_recv.at[at, p], device_id=target, device_id_type=MESH,
        )

    def to_up(p):
        return copy(right, from_low, 0, p, (g, d + 1))

    def to_down(p):
        return copy(left, from_high, 1, p, (g, d - 1))

    def to_far():
        return copy(right, from_far, 2, 0, (g, d + 2))

    pl.when(far[0])(lambda: to_far().start())

    @pl.loop(0, rb)
    def _(p):
        pl.when(up[0])(lambda: to_up(p).start())
        pl.when(down[0])(lambda: to_down(p).start())

    def prepare(p):
        mine_sum[p] = own[p]

        @pl.when(up[1])
        def _():
            to_up(p).wait_recv()
            mine_sum[p] = mine_sum[p] + from_low[p].astype(jnp.float32)

        @pl.when(down[1])
        def _():
            to_down(p).wait_recv()
            mine_sum[p] = mine_sum[p] + from_high[p].astype(jnp.float32)

        @pl.when(far[1] & (p == 0))
        def _():
            to_far().wait_recv()
            mine_sum[p] = mine_sum[p] + from_far[0].astype(jnp.float32)

        present = trial[p].astype(jnp.float32)
        mine[p] = ((mine_sum[p] - CENTER * present) / HALFWIDTH).astype(mine.dtype)

    mine_sum, sems = sems[0], sems[1:]
    spread(mine, window, rb, n_grp, n_dev, low, high, sems, prepare)

    @pl.loop(0, rb)
    def _(p):
        pl.when(up[0])(lambda: to_up(p).wait_send())
        pl.when(down[0])(lambda: to_down(p).wait_send())

    pl.when(far[0])(lambda: to_far().wait_send())


def fetch(sizes, blocks, window, held, near, sems):
    rb, n_grp, n_dev, low, high = sizes
    d = lax.axis_index("dev")
    base = (n_dev + d - low) * rb
    rows = pltpu.make_async_copy(window.at[pl.ds(base, near.shape[0])], near, sems.at[CHUNKS])
    rows.start()
    size = blocks.shape[0] // CHUNKS

    def part(c):
        here = pl.ds(c * size, size)
        return pltpu.make_async_copy(blocks.at[here], held.at[here], sems.at[c])

    for c in range(CHUNKS):
        part(c).start()
    rows.wait()

    def ready(begin, end):
        for c in range(CHUNKS):
            pl.when((begin <= c * size) & (end > c * size))(lambda: part(c).wait())

    return base, ready


def bounds(pointer, row, first_nnz, nnz_here):
    count = pointer.shape[1] - 1
    at = jnp.clip(row, 0, count - 1)
    begin = jnp.clip(pointer[0, at] - first_nnz, 0, nnz_here)
    end = jnp.clip(pointer[0, at + 1] - first_nnz, 0, nnz_here)
    return begin, jnp.where((row >= 0) & (row < count), end, begin)


def row_sum(begin, end, shift, offsets, held, near):
    def step(i, total):
        lhs, rhs = [], []
        for j in range(DEPTH):
            b = begin + i * DEPTH + j
            valid = b < end
            b = jnp.minimum(b, end - 1)
            block = held[b]
            lhs.append(jnp.where(valid, block, jnp.zeros_like(block)))
            rhs.append(near[offsets[0, b] + shift])
        return total + jnp.dot(
            jnp.concatenate(lhs, axis=1), jnp.concatenate(rhs, axis=0), preferred_element_type=jnp.float32
        )

    turns = (end - begin + DEPTH - 1) // DEPTH
    return lax.fori_loop(0, turns, step, jnp.zeros(near.shape[1:], jnp.float32))


def frame_kernel(sizes, pointer, offsets, blocks, window, left, own, right, held, near, sems):
    rb, n_grp, n_dev, low, high = sizes
    nnz_here = blocks.shape[0]
    d = lax.axis_index("dev")
    base, ready = fetch(sizes, blocks, window, held, near, sems)

    def one(at):
        row = (d - 1) * rb + at
        begin, end = bounds(pointer, row, d * nnz_here, nnz_here)
        ready(begin, end)
        return row_sum(begin, end, row + n_dev * rb - base, offsets, held, near)

    @pl.loop(0, rb)
    def _(at):
        left[at] = one(at).astype(left.dtype)

    @pl.loop(0, rb)
    def _(at):
        own[at] = one(rb + at)

    @pl.loop(0, rb + 1)
    def _(at):
        right[at] = one(2 * rb + at).astype(right.dtype)


def slots_kernel(sizes, pointer, offsets, blocks, window, before, filtered, head, tail, held, near, older, sems):
    rb, n_grp, n_dev, low, high = sizes
    nnz_here = blocks.shape[0]
    d = lax.axis_index("dev")
    first_nnz = d * nnz_here
    band_rows = pointer.shape[1] - 1

    def count(limit):
        def add(r, total):
            return total + jnp.where(pointer[0, r + 1] <= limit, 1, 0)

        return lax.fori_loop(0, band_rows, add, jnp.int32(0))

    first = count(first_nnz)
    finished = count(first_nnz + nnz_here) - first
    past = pltpu.make_async_copy(before.at[pl.ds(band_rows + first, SPAN)], older, sems.at[CHUNKS + 1])
    past.start()
    base, ready = fetch(sizes, blocks, window, held, near, sems)
    past.wait()

    def one(row):
        begin, end = bounds(pointer, row, first_nnz, nnz_here)
        ready(begin, end)
        return row_sum(begin, end, row + band_rows - base, offsets, held, near)

    @pl.loop(0, SPAN)
    def _(slot):
        filled = slot < finished
        row = first + slot

        @pl.when(filled)
        def _():
            present = near[row + band_rows - base].astype(jnp.float32)
            value = 2.0 * (one(row) - CENTER * present) / HALFWIDTH - older[slot].astype(jnp.float32)
            filtered[slot] = value.astype(filtered.dtype)

            @pl.when(slot == 0)
            def _():
                head[0] = value

        @pl.when(jnp.logical_not(filled))
        def _():
            filtered[slot] = jnp.zeros(filtered.shape[1:], filtered.dtype)

    tail[0] = one(first + finished).astype(tail.dtype)


def local(n_grp, n_dev, row_ptr, col_off, blocks, trial):
    nnz_here, blk, _ = blocks.shape
    vectors = trial.shape[1]
    band_rows = row_ptr.shape[1] - 1
    rb = band_rows // n_dev
    half = max(FLOOR, band_rows // 2)
    reach = -(-half // rb)
    low, high = 1 + reach, 2 + reach
    _, y_count = grid_of(n_dev)
    own_rows = trial.reshape(rb, blk, vectors)
    sizes = (rb, n_grp, n_dev, low, high)
    near_rows = (low + high) * rb + 1
    dma = pltpu.SemaphoreType.DMA
    sems = [
        dma((n_dev, rb)), dma((2, n_dev)), dma((2, n_dev)), dma((max(1, y_count - 1), n_dev)), dma((2, n_dev)), dma,
    ]
    any_spec = pl.BlockSpec(memory_space=pl.ANY)
    vmem = pl.BlockSpec(memory_space=pltpu.VMEM)
    smem = pl.BlockSpec(memory_space=pltpu.SMEM)
    kept = trial.dtype

    def shape(rows, dtype):
        return jax.ShapeDtypeStruct((rows, blk, vectors), dtype)

    def buffer(rows, dtype):
        return pltpu.VMEM((rows, blk, vectors), dtype)

    def remote(collective_id):
        return pltpu.CompilerParams(
            collective_id=collective_id, has_side_effects=True, vmem_limit_bytes=VMEM_BYTES
        )

    here = pltpu.CompilerParams(vmem_limit_bytes=VMEM_BYTES)
    first = pl.pallas_call(
        functools.partial(first_kernel, sizes),
        out_shape=shape(3 * band_rows, kept),
        in_specs=[any_spec],
        out_specs=any_spec,
        scratch_shapes=sems,
        compiler_params=remote(0),
        name="spread_trial",
    )(own_rows)
    left, own, right = pl.pallas_call(
        functools.partial(frame_kernel, sizes),
        out_shape=(shape(rb, kept), shape(rb, jnp.float32), shape(rb + 1, kept)),
        in_specs=[smem] * 2 + [any_spec] * 2,
        out_specs=(vmem, vmem, vmem),
        scratch_shapes=[pltpu.VMEM(blocks.shape, blocks.dtype), buffer(near_rows, kept), dma((CHUNKS + 1,))],
        compiler_params=here,
        name="sums_first",
    )(row_ptr, col_off, blocks, first)
    second = pl.pallas_call(
        functools.partial(second_kernel, sizes),
        out_shape=shape(3 * band_rows, kept),
        in_specs=[vmem] * 4,
        out_specs=any_spec,
        scratch_shapes=[buffer(rb, kept)] * 3 + [buffer(1, kept), dma((3, rb)), dma((3, rb)), buffer(rb, jnp.float32)] + sems,
        compiler_params=remote(1),
        name="finish_and_spread",
    )(left, own, right, own_rows)
    filtered, head, tail = pl.pallas_call(
        functools.partial(slots_kernel, sizes),
        out_shape=(shape(SPAN, kept), shape(1, jnp.float32), shape(1, kept)),
        in_specs=[smem] * 2 + [any_spec] * 3,
        out_specs=(vmem, vmem, vmem),
        scratch_shapes=[
            pltpu.VMEM(blocks.shape, blocks.dtype), buffer(near_rows, kept), buffer(SPAN, kept), dma((CHUNKS + 2,)),
        ],
        compiler_params=here,
        name="sums_second",
    )(row_ptr, col_off, blocks, second, first)
    carried = lax.ppermute(tail, "dev", [(i, i + 1) for i in range(n_dev - 1)])
    start = (head + carried.astype(jnp.float32) * (2.0 / HALFWIDTH)).astype(kept)
    filtered = lax.dynamic_update_slice_in_dim(filtered, start, 0, 0)
    return filtered.reshape(SPAN * blk, vectors)


def solution(mesh):
    in_specs = (
        P("grp", None),
        P("grp", "dev"),
        P(("grp", "dev"), None, None),
        P(("grp", "dev"), None),
    )
    step = functools.partial(local, mesh.shape["grp"], mesh.shape["dev"])
    return jax.shard_map(step, mesh=mesh, in_specs=in_specs, out_specs=P(("grp", "dev"), None), check_vma=False)
```

```python
import functools

import jax
import jax.numpy as jnp
from jax import lax
from jax.experimental import pallas as pl
from jax.experimental.pallas import tpu as pltpu
from jax.sharding import PartitionSpec as P

SPAN = 6
CENTER = 0.5
HALFWIDTH = 1.5
FLOOR = 24
DEPTH = 24
CHUNKS = 4
VMEM_BYTES = 56 * 1024 * 1024
MESH = pl.DeviceIdType.MESH


def grid_of(n_dev):
    z_count = 1
    while z_count * z_count < n_dev:
        z_count *= 2
    return z_count, n_dev // z_count


def spread(mine, window, rb, n_grp, n_dev, low, high, sems, prepare=None):
    recv_own, recv_side, send_z, send_y, send_side, local_sem = sems
    z_count, y_count = grid_of(n_dev)
    g, d = lax.axis_index("grp"), lax.axis_index("dev")
    z, y = d // y_count, lax.rem(d, y_count)
    after = lax.rem(g + 1, n_grp)
    before = lax.rem(g + n_grp - 1, n_grp)
    early = rb // 4 if y_count > 1 and prepare is not None else 0

    def rows(slot, p=None, count=1):
        return window.at[pl.ds(slot * rb, rb)] if p is None else window.at[pl.ds(slot * rb + p, count)]

    def post(cond, src, dst, send_sem, recv_sem, target):
        @pl.when(cond)
        def _():
            pltpu.make_async_remote_copy(
                src_ref=src, dst_ref=dst, send_sem=send_sem, recv_sem=recv_sem, device_id=target, device_id_type=MESH
            ).start()

    def drain(cond, ref, sem):
        @pl.when(cond)
        def _():
            pltpu.make_async_copy(ref, ref, sem).wait()

    def to_sides(cond, s, p, src):
        post(cond & (s >= d + n_dev - low), src, rows(s, p), send_side.at[0, s], recv_side.at[0, s], (after, d))
        post(
            cond & ((s <= d + high - 1 - n_dev) | ((s == d + high - n_dev) & (p == 0))), src, rows(2 * n_dev + s, p),
            send_side.at[1, s], recv_side.at[1, s], (before, d),
        )

    def along(cond, s, p, way, src):
        dst = rows(n_dev + s, p)
        if way >= 0:
            post(cond & (z < z_count - 1), src, dst, send_z.at[0, s], recv_own.at[s, p], (g, d + y_count))
        if way <= 0:
            post(cond & (z > 0), src, dst, send_z.at[1, s], recv_own.at[s, p], (g, d - y_count))

    def line_step(cond, s, p, way, src):
        along(cond, s, p, way, src)
        for step in range(1, y_count):
            other = z * y_count + lax.rem(y + step, y_count)
            post(
                cond if way == 0 else cond & (p >= early), src, rows(n_dev + s, p),
                send_y.at[step - 1, s], recv_own.at[s, p], (g, other),
            )
        to_sides(cond, s, p, src)

    def around(k):
        if k == 0:
            return [(z >= 0, z, 0)]
        return [(z - k >= 0, z - k, 1), (z + k < z_count, z + k, -1)]

    def across(k, p):
        for cond, at, way in around(k):
            at = jnp.clip(at, 0, z_count - 1)
            for step in range(1, y_count):
                s = at * y_count + lax.rem(y + step, y_count)
                drain(cond, rows(n_dev + s, p), recv_own.at[s, p])
                along(cond & (p < early), s, p, way, rows(n_dev + s, p))
                to_sides(cond, s, p, rows(n_dev + s, p))

    @pl.loop(0, rb)
    def _(p):
        if prepare is not None:
            prepare(p)
        line_step(z >= 0, d, p, 0, mine.at[pl.ds(p, 1)])

    keep = pltpu.make_async_copy(mine, rows(n_dev + d), local_sem)
    keep.start()

    for k in range(1, z_count + 1):
        @pl.loop(0, rb)
        def _(p, k=k):
            if k < z_count:
                for cond, at, way in around(k):
                    s = jnp.clip(at, 0, z_count - 1) * y_count + y
                    drain(cond, rows(n_dev + s, p), recv_own.at[s, p])
                    line_step(cond, s, p, way, rows(n_dev + s, p))
            across(k - 1, p)

    @pl.loop(0, n_dev)
    def _(s):
        s_z, s_y = s // y_count, lax.rem(s, y_count)
        low_in, high_in, edge_in = s >= d + n_dev - low, s <= d + high - 1 - n_dev, s == d + high - n_dev
        shard, later = rows(s), rows(2 * n_dev + s)
        one = rows(2 * n_dev + s, 0)
        drain(low_in, shard, recv_side.at[0, s])
        drain(high_in, later, recv_side.at[1, s])
        drain(edge_in, one, recv_side.at[1, s])
        drain(low_in, shard, send_side.at[0, s])
        drain(high_in, later, send_side.at[1, s])
        drain(edge_in, one, send_side.at[1, s])
        first, rest = window.at[pl.ds(s * rb, max(1, early))], window.at[pl.ds(s * rb, rb - early)]
        line = s_y == y
        for way, cond in ((0, (s_z <= z) & (z < z_count - 1)), (1, (s_z >= z) & (z > 0))):
            drain(cond & line, shard, send_z.at[way, s])
            if early:
                drain(cond & jnp.logical_not(line), first, send_z.at[way, s])
        for step in range(1, y_count):
            drain(s == d, shard, send_y.at[step - 1, s])
            drain(line & (s != d), rest, send_y.at[step - 1, s])

    keep.wait()


def greet(n_grp, n_dev, partials):
    _, y_count = grid_of(n_dev)
    z_count = n_dev // y_count
    g, d = lax.axis_index("grp"), lax.axis_index("dev")
    z, y = d // y_count, lax.rem(d, y_count)
    barrier = pltpu.get_barrier_semaphore()
    expected = jnp.int32(0)
    targets = [
        (z >= 0, (lax.rem(g + 1, n_grp), d)),
        (z >= 0, (lax.rem(g + n_grp - 1, n_grp), d)),
        (z < z_count - 1, (g, d + y_count)),
        (z > 0, (g, d - y_count)),
    ]
    for step in range(1, y_count):
        targets.append((z >= 0, (g, z * y_count + lax.rem(y + step, y_count))))
    if partials:
        for by in (1, 2):
            targets.append((d + by < n_dev, (g, d + by)))
            targets.append((d - by >= 0, (g, d - by)))
    for cond, target in targets:
        @pl.when(cond)
        def _(target=target):
            pl.semaphore_signal(barrier, inc=1, device_id=target, device_id_type=MESH)

        expected = expected + jnp.where(cond, 1, 0)
    pl.semaphore_wait(barrier, expected)


def first_kernel(sizes, trial, window, *sems):
    rb, n_grp, n_dev, low, high = sizes
    greet(n_grp, n_dev, False)
    spread(trial, window, rb, n_grp, n_dev, low, high, sems)


def second_kernel(sizes, left, own, right, trial, window, mine, from_low, from_high, from_far, part_send, part_recv, *sems):
    rb, n_grp, n_dev, low, high = sizes
    greet(n_grp, n_dev, True)
    g, d = lax.axis_index("grp"), lax.axis_index("dev")
    up, down, far = (d < n_dev - 1, d > 0), (d > 0, d < n_dev - 1), (d < n_dev - 2, d > 1)

    def copy(src, dst, at, p, target):
        return pltpu.make_async_remote_copy(
            src_ref=src.at[pl.ds(p if at < 2 else rb, 1)], dst_ref=dst.at[pl.ds(p, 1)],
            send_sem=part_send.at[at, p], recv_sem=part_recv.at[at, p], device_id=target, device_id_type=MESH,
        )

    def to_up(p):
        return copy(right, from_low, 0, p, (g, d + 1))

    def to_down(p):
        return copy(left, from_high, 1, p, (g, d - 1))

    def to_far():
        return copy(right, from_far, 2, 0, (g, d + 2))

    pl.when(far[0])(lambda: to_far().start())

    @pl.loop(0, rb)
    def _(p):
        pl.when(up[0])(lambda: to_up(p).start())
        pl.when(down[0])(lambda: to_down(p).start())

    def prepare(p):
        mine_sum[p] = own[p]

        @pl.when(up[1])
        def _():
            to_up(p).wait_recv()
            mine_sum[p] = mine_sum[p] + from_low[p].astype(jnp.float32)

        @pl.when(down[1])
        def _():
            to_down(p).wait_recv()
            mine_sum[p] = mine_sum[p] + from_high[p].astype(jnp.float32)

        @pl.when(far[1] & (p == 0))
        def _():
            to_far().wait_recv()
            mine_sum[p] = mine_sum[p] + from_far[0].astype(jnp.float32)

        present = trial[p].astype(jnp.float32)
        mine[p] = ((mine_sum[p] - CENTER * present) / HALFWIDTH).astype(mine.dtype)

    mine_sum, sems = sems[0], sems[1:]
    spread(mine, window, rb, n_grp, n_dev, low, high, sems, prepare)

    @pl.loop(0, rb)
    def _(p):
        pl.when(up[0])(lambda: to_up(p).wait_send())
        pl.when(down[0])(lambda: to_down(p).wait_send())

    pl.when(far[0])(lambda: to_far().wait_send())


def fetch(sizes, blocks, window, held, near, sems):
    rb, n_grp, n_dev, low, high = sizes
    d = lax.axis_index("dev")
    base = (n_dev + d - low) * rb
    rows = pltpu.make_async_copy(window.at[pl.ds(base, near.shape[0])], near, sems.at[CHUNKS])
    rows.start()
    size = blocks.shape[0] // CHUNKS

    def part(c):
        here = pl.ds(c * size, size)
        return pltpu.make_async_copy(blocks.at[here], held.at[here], sems.at[c])

    for c in range(CHUNKS):
        part(c).start()
    rows.wait()

    def ready(begin, end):
        for c in range(CHUNKS):
            pl.when((begin <= c * size) & (end > c * size))(lambda: part(c).wait())

    return base, ready


def bounds(pointer, row, first_nnz, nnz_here):
    count = pointer.shape[1] - 1
    at = jnp.clip(row, 0, count - 1)
    begin = jnp.clip(pointer[0, at] - first_nnz, 0, nnz_here)
    end = jnp.clip(pointer[0, at + 1] - first_nnz, 0, nnz_here)
    return begin, jnp.where((row >= 0) & (row < count), end, begin)


def row_sum(begin, end, shift, offsets, held, near):
    def step(i, total):
        lhs, rhs = [], []
        for j in range(DEPTH):
            b = begin + i * DEPTH + j
            valid = b < end
            b = jnp.minimum(b, end - 1)
            block = held[b]
            lhs.append(jnp.where(valid, block, jnp.zeros_like(block)))
            rhs.append(near[offsets[0, b] + shift])
        return total + jnp.dot(
            jnp.concatenate(lhs, axis=1), jnp.concatenate(rhs, axis=0), preferred_element_type=jnp.float32
        )

    turns = (end - begin + DEPTH - 1) // DEPTH
    return lax.fori_loop(0, turns, step, jnp.zeros(near.shape[1:], jnp.float32))


def frame_kernel(sizes, pointer, offsets, blocks, window, left, own, right, held, near, sems):
    rb, n_grp, n_dev, low, high = sizes
    nnz_here = blocks.shape[0]
    d = lax.axis_index("dev")
    base, ready = fetch(sizes, blocks, window, held, near, sems)

    def one(at):
        row = (d - 1) * rb + at
        begin, end = bounds(pointer, row, d * nnz_here, nnz_here)
        ready(begin, end)
        return row_sum(begin, end, row + n_dev * rb - base, offsets, held, near)

    @pl.loop(0, rb)
    def _(at):
        left[at] = one(at).astype(left.dtype)

    @pl.loop(0, rb)
    def _(at):
        own[at] = one(rb + at)

    @pl.loop(0, rb + 1)
    def _(at):
        right[at] = one(2 * rb + at).astype(right.dtype)


def slots_kernel(sizes, pointer, offsets, blocks, window, before, filtered, head, tail, held, near, older, sems):
    rb, n_grp, n_dev, low, high = sizes
    nnz_here = blocks.shape[0]
    d = lax.axis_index("dev")
    first_nnz = d * nnz_here
    band_rows = pointer.shape[1] - 1

    def count(limit):
        def add(r, total):
            return total + jnp.where(pointer[0, r + 1] <= limit, 1, 0)

        return lax.fori_loop(0, band_rows, add, jnp.int32(0))

    first = count(first_nnz)
    finished = count(first_nnz + nnz_here) - first
    past = pltpu.make_async_copy(before.at[pl.ds(band_rows + first, SPAN)], older, sems.at[CHUNKS + 1])
    past.start()
    base, ready = fetch(sizes, blocks, window, held, near, sems)
    past.wait()

    def one(row):
        begin, end = bounds(pointer, row, first_nnz, nnz_here)
        ready(begin, end)
        return row_sum(begin, end, row + band_rows - base, offsets, held, near)

    @pl.loop(0, SPAN)
    def _(slot):
        filled = slot < finished
        row = first + slot

        @pl.when(filled)
        def _():
            present = near[row + band_rows - base].astype(jnp.float32)
            value = 2.0 * (one(row) - CENTER * present) / HALFWIDTH - older[slot].astype(jnp.float32)
            filtered[slot] = value.astype(filtered.dtype)

            @pl.when(slot == 0)
            def _():
                head[0] = value

        @pl.when(jnp.logical_not(filled))
        def _():
            filtered[slot] = jnp.zeros(filtered.shape[1:], filtered.dtype)

    tail[0] = one(first + finished).astype(tail.dtype)


def local(n_grp, n_dev, row_ptr, col_off, blocks, trial):
    nnz_here, blk, _ = blocks.shape
    vectors = trial.shape[1]
    band_rows = row_ptr.shape[1] - 1
    rb = band_rows // n_dev
    half = max(FLOOR, band_rows // 2)
    reach = -(-half // rb)
    low, high = 1 + reach, 2 + reach
    _, y_count = grid_of(n_dev)
    own_rows = trial.reshape(rb, blk, vectors)
    sizes = (rb, n_grp, n_dev, low, high)
    near_rows = (low + high) * rb + 1
    dma = pltpu.SemaphoreType.DMA
    sems = [
        dma((n_dev, rb)), dma((2, n_dev)), dma((2, n_dev)), dma((max(1, y_count - 1), n_dev)), dma((2, n_dev)), dma,
    ]
    any_spec = pl.BlockSpec(memory_space=pl.ANY)
    vmem = pl.BlockSpec(memory_space=pltpu.VMEM)
    smem = pl.BlockSpec(memory_space=pltpu.SMEM)
    kept = trial.dtype

    def shape(rows, dtype):
        return jax.ShapeDtypeStruct((rows, blk, vectors), dtype)

    def buffer(rows, dtype):
        return pltpu.VMEM((rows, blk, vectors), dtype)

    def remote(collective_id):
        return pltpu.CompilerParams(
            collective_id=collective_id, has_side_effects=True, vmem_limit_bytes=VMEM_BYTES
        )

    here = pltpu.CompilerParams(vmem_limit_bytes=VMEM_BYTES)
    first = pl.pallas_call(
        functools.partial(first_kernel, sizes),
        out_shape=shape(3 * band_rows, kept),
        in_specs=[any_spec],
        out_specs=any_spec,
        scratch_shapes=sems,
        compiler_params=remote(0),
        name="spread_trial",
    )(own_rows)
    left, own, right = pl.pallas_call(
        functools.partial(frame_kernel, sizes),
        out_shape=(shape(rb, kept), shape(rb, jnp.float32), shape(rb + 1, kept)),
        in_specs=[smem] * 2 + [any_spec] * 2,
        out_specs=(vmem, vmem, vmem),
        scratch_shapes=[pltpu.VMEM(blocks.shape, blocks.dtype), buffer(near_rows, kept), dma((CHUNKS + 1,))],
        compiler_params=here,
        name="sums_first",
    )(row_ptr, col_off, blocks, first)
    second = pl.pallas_call(
        functools.partial(second_kernel, sizes),
        out_shape=shape(3 * band_rows, kept),
        in_specs=[vmem] * 4,
        out_specs=any_spec,
        scratch_shapes=[buffer(rb, kept)] * 3 + [buffer(1, kept), dma((3, rb)), dma((3, rb)), buffer(rb, jnp.float32)] + sems,
        compiler_params=remote(1),
        name="finish_and_spread",
    )(left, own, right, own_rows)
    filtered, head, tail = pl.pallas_call(
        functools.partial(slots_kernel, sizes),
        out_shape=(shape(SPAN, kept), shape(1, jnp.float32), shape(1, kept)),
        in_specs=[smem] * 2 + [any_spec] * 3,
        out_specs=(vmem, vmem, vmem),
        scratch_shapes=[
            pltpu.VMEM(blocks.shape, blocks.dtype), buffer(near_rows, kept), buffer(SPAN, kept), dma((CHUNKS + 2,)),
        ],
        compiler_params=here,
        name="sums_second",
    )(row_ptr, col_off, blocks, second, first)
    carried = lax.ppermute(tail, "dev", [(i, i + 1) for i in range(n_dev - 1)])
    start = (head + carried.astype(jnp.float32) * (2.0 / HALFWIDTH)).astype(kept)
    filtered = lax.dynamic_update_slice_in_dim(filtered, start, 0, 0)
    return filtered.reshape(SPAN * blk, vectors)


def solution(mesh):
    in_specs = (
        P("grp", None),
        P("grp", "dev"),
        P(("grp", "dev"), None, None),
        P(("grp", "dev"), None),
    )
    step = functools.partial(local, mesh.shape["grp"], mesh.shape["dev"])
    return jax.shard_map(step, mesh=mesh, in_specs=in_specs, out_specs=P(("grp", "dev"), None), check_vma=False)
```
